32 devices in a mesh: clip: 4 (over x, core), frame: 8 (over z, y).
Axes of the slice: x: 2, y: 2, z: 4, core: 2. Of those that a mesh axis runs over, the one named last changes fastest.
Arguments:
- video_tokens: bfloat16 [8, 32, 256, 1024], P('clip', 'frame'), parts along dimension 0, may hold values from -6 to 6
- frame_count: int32 [8], P('clip'), parts along dimension 0, may hold values from 8 to 32, as said below
- token_count: int32 [8], P('clip'), parts along dimension 0, may hold values from 128 to 256, as said below
- time_gain: float32 [1024], replicated, may hold values from 0.5 to 2
- time_qkv: bfloat16 [1024, 1536], replicated
- time_out: bfloat16 [512, 1024], replicated, may hold values from -0.5 to 0.5
- space_gain: float32 [1024], replicated, may hold values from 0.5 to 2
- space_qkv: bfloat16 [1024, 1536], replicated
- space_out: bfloat16 [512, 1024], replicated, may hold values from -0.5 to 0.5
Outputs:
- block_out: bfloat16 [8, 32, 256, 1024], P('clip', 'frame'), parts along dimension 0
The draws below stay inside these ranges and needn't reach their ends.
There are 4 independent parts, one for each index of `clip`. The reference program is written for one: setup_inputs(seed, part) draws one part's arguments, and reference() takes and returns one part's arrays. A program takes and returns all parts, laid end to end along the dimension named above; an argument that names none is the same for every part. Nothing has to cross between parts.
Inputs may be any that keep to these rules, and one draw needn't show every extreme that they name: `frame_count`: frames of each clip; in every draw some clip has all 32. `token_count`: tokens of each frame; in every draw some clip has all 256.
All inputs are finite; a program needn't handle non-finite values.
Results may differ from the reference program's by a relative error of at most 0.025.
The reference program's roundings to bfloat16 on the way count: a program that leaves them out, or rounds other values in their place, can miss the bound.
Values may be sent and summed in bfloat16 or wider, within the bound.
No kernel may reach another device: no remote copies, remote signals or barrier semaphores. Data moves between devices by JAX's collectives and lax.ppermute only.
A program may use at most 128 MiB of HBM per device.

```python
import math
import jax
import jax.numpy as jnp
from jax import lax

D = 1024
HEADS = 8
HD = 64
HW = 512
TOKP = 256
CLIPS = 2
FRAMES = 32


def fresh_projection(key, head_factor):
    first_key, second_key, third_key = jax.random.split(key, 3)
    queries = jax.random.normal(first_key, (D, HW), jnp.float32) * D ** (-0.5)
    keys_part = jax.random.normal(second_key, (D, HW), jnp.float32) * D ** (-0.5)
    values = jax.random.normal(third_key, (D, HW), jnp.float32) * D ** (-0.5)
    column_factor = jnp.repeat(head_factor, HD)[None, :]
    queries = queries * column_factor
    keys_part = keys_part * column_factor
    return jnp.concatenate([queries, keys_part, values], axis=1).astype(jnp.bfloat16)


def draw_time_qkv(key, part):
    key = jax.random.fold_in(key, 11)
    weight_key = jax.random.fold_in(key, 1)
    return fresh_projection(weight_key, jnp.ones((HEADS,), jnp.float32))


def draw_space_qkv(key, part):
    key = jax.random.fold_in(key, 13)
    weight_key = jax.random.fold_in(key, 1)
    return fresh_projection(weight_key, jnp.ones((HEADS,), jnp.float32))


def draw_frame_count(key, part):
    key = jax.random.fold_in(key, 3)
    first_key, second_key = jax.random.split(key)
    counts = jax.random.randint(first_key, (CLIPS,), FRAMES // 4, FRAMES + 1)
    chosen = jax.random.randint(second_key, (), 0, CLIPS)
    return jnp.where(jnp.arange(CLIPS) == chosen, FRAMES, counts).astype(jnp.int32)


def draw_token_count(key, part):
    key = jax.random.fold_in(key, 5)
    first_key, second_key = jax.random.split(key)
    counts = jax.random.randint(first_key, (CLIPS,), TOKP // 2, TOKP + 1)
    chosen = jax.random.randint(second_key, (), 0, CLIPS)
    return jnp.where(jnp.arange(CLIPS) == chosen, TOKP, counts).astype(jnp.int32)


def level_of(key, shape, shards, low, top_value):
    level = 1.0
    for position, blocks in shards:
        steps = jax.random.uniform(jax.random.fold_in(jax.random.fold_in(key, 6), position), (blocks,), jnp.float32, low / len(shards), top_value / len(shards))
        level = level * jnp.repeat(jnp.exp(steps), shape[position] // blocks).reshape((-1,) + (1,) * (len(shape) - 1 - position))
    return level


def normal_values(key, dims, width, reach, shards=(), held_as=jnp.bfloat16):
    level = level_of(key, dims, shards, -0.22, 0.18) if shards else 1.0
    array = jax.random.normal(key, dims, jnp.float32) * width * level
    return jnp.minimum(jnp.maximum(array, -reach), reach).astype(held_as)


def setup_inputs(seed: int = 0, part: int = 0) -> dict:
    arg_keys = jax.random.split(jax.random.key(seed), 10)
    own_keys = jax.random.split(jax.random.fold_in(arg_keys[9], part), 10)
    return {
        "video_tokens": normal_values(own_keys[0], (CLIPS, FRAMES, TOKP, D), 1.0, 6.0, ((1, 8),)),
        "frame_count": draw_frame_count(jax.random.fold_in(jax.random.fold_in(arg_keys[9], part), 71), part),
        "token_count": draw_token_count(jax.random.fold_in(jax.random.fold_in(arg_keys[9], part), 71), part),
        "time_gain": jnp.clip(jnp.exp(jax.random.uniform(arg_keys[3], (D,), jnp.float32, math.log(0.5), math.log(2.0))), 0.5, 2.0),
        "time_qkv": draw_time_qkv(jax.random.fold_in(arg_keys[9], 71), part),
        "time_out": normal_values(arg_keys[5], (HW, D), (HW // 4) ** -0.5, 0.5),
        "space_gain": jnp.clip(jnp.exp(jax.random.uniform(arg_keys[6], (D,), jnp.float32, math.log(0.5), math.log(2.0))), 0.5, 2.0),
        "space_qkv": draw_space_qkv(jax.random.fold_in(arg_keys[9], 71), part),
        "space_out": normal_values(arg_keys[8], (HW, D), (HW // 4) ** -0.5, 0.5),
    }


def layer_norm(row_block, row_gain):
    values = row_block.astype(jnp.float32)
    centre = values - lax.optimization_barrier(jnp.mean(values, axis=-1, keepdims=True))
    spread = lax.optimization_barrier(jnp.mean(centre * centre, axis=-1, keepdims=True))
    return (centre * lax.rsqrt(spread + 1e-05) * row_gain).astype(jnp.bfloat16)

def project(row_block, weight):
    dims_in = row_block.shape
    flattened = row_block.reshape(-1, dims_in[-1])
    result = jnp.dot(flattened, weight, preferred_element_type=jnp.float32)
    return result.reshape(dims_in[:-1] + (weight.shape[1],))

def attend_weights(scores, key_valid):
    masked = jnp.where(key_valid, scores, jnp.float32(-1e+30))
    peak = lax.optimization_barrier(jnp.max(masked, axis=-1, keepdims=True))
    expo = jnp.exp(masked - peak)
    return (expo / lax.optimization_barrier(jnp.sum(expo, axis=-1, keepdims=True))).astype(jnp.bfloat16)

def reference(video_tokens, frame_count, token_count, time_gain, time_qkv, time_out, space_gain, space_qkv, space_out):
    clip_count, frames, tokens, row_width = video_tokens.shape
    score_scale = HD ** (-0.5)
    frame_live = jnp.arange(frames)[None, :] < frame_count[:, None]
    token_live = jnp.arange(tokens)[None, :] < token_count[:, None]
    normed = layer_norm(video_tokens, time_gain)
    projected = project(normed, time_qkv).astype(jnp.bfloat16)
    projected = projected.reshape(clip_count, frames, tokens, 3, HEADS, HD).astype(jnp.float32)
    scores = jnp.einsum('cfphd,cgphd->cphfg', projected[:, :, :, 0], projected[:, :, :, 1]) * score_scale
    weights = attend_weights(scores, frame_live[:, None, None, None, :])
    attended = jnp.einsum('cphfg,cgphd->cfphd', weights.astype(jnp.float32), projected[:, :, :, 2])
    attended = attended.astype(jnp.bfloat16).reshape(clip_count, frames, tokens, HW)
    middle = (video_tokens.astype(jnp.float32) + project(attended, time_out)).astype(jnp.bfloat16)

    def spatial(clip_item):
        row_block, limit = clip_item
        normed_s = layer_norm(row_block, space_gain)
        proj_s = project(normed_s, space_qkv).astype(jnp.bfloat16)
        proj_s = proj_s.reshape(frames, tokens, 3, HEADS, HD).astype(jnp.float32)
        scores_s = jnp.einsum('fphd,fqhd->fhpq', proj_s[:, :, 0], proj_s[:, :, 1]) * score_scale
        key_valid = (jnp.arange(tokens) < limit)[None, None, None, :]
        weights_s = attend_weights(scores_s, key_valid)
        att_s = jnp.einsum('fhpq,fqhd->fphd', weights_s.astype(jnp.float32), proj_s[:, :, 2])
        att_s = att_s.astype(jnp.bfloat16).reshape(frames, tokens, HW)
        return project(att_s, space_out)
    branch = lax.map(spatial, (middle, token_count))
    live = frame_live[:, :, None] & token_live[:, None, :]
    summed = middle.astype(jnp.float32) + branch
    return jnp.where(live[..., None], summed, jnp.float32(0.0)).astype(jnp.bfloat16)
```

```python
import functools

import jax
import jax.numpy as jnp
from jax import lax
from jax.experimental import pallas as pl
from jax.experimental.pallas import tpu as pltpu
from jax.sharding import PartitionSpec as P

HEADS = 8
HD = 64
HW = 512
ROWS = 16
NEG = -1e30
VMEM_LIMIT = 50 * 1024 * 1024
ANY = pl.BlockSpec(memory_space=pl.ANY)


def normalise(values, gain):
    centre = values - jnp.mean(values, axis=-1, keepdims=True)
    spread = jnp.mean(centre * centre, axis=-1, keepdims=True)
    return (centre * lax.rsqrt(spread + 1e-05) * gain).astype(jnp.bfloat16)


def attend(qkv_ref, rows, bias, out_ref):
    count = rows.size
    low = lax.broadcasted_iota(jnp.int32, (count, 2 * HD), 1) < HD
    zero = jnp.zeros((count, 2 * HD), jnp.bfloat16)
    for pair in range(HEADS // 2):
        cols = pair * 2 * HD
        q = qkv_ref[rows, cols : cols + 2 * HD]
        k = qkv_ref[rows, HW + cols : HW + cols + 2 * HD]
        v = qkv_ref[rows, 2 * HW + cols : 2 * HW + cols + 2 * HD]
        parts = []
        for keys in (jnp.where(low, k, zero), jnp.where(low, zero, k)):
            scores = lax.dot_general(q, keys, (((1,), (1,)), ((), ())), preferred_element_type=jnp.float32)
            scores = scores + bias
            expo = jnp.exp(scores - jnp.max(scores, axis=-1, keepdims=True))
            weights = (expo * (1.0 / jnp.sum(expo, axis=-1, keepdims=True))).astype(jnp.bfloat16)
            parts.append(jnp.dot(weights, v, preferred_element_type=jnp.float32))
        out_ref[rows, cols : cols + 2 * HD] = jnp.where(low, parts[0], parts[1]).astype(jnp.bfloat16)


def project_heads(normed, weight_ref, qkv_ref):
    for part in range(3):
        result = jnp.dot(normed, weight_ref[:, part * HW : (part + 1) * HW], preferred_element_type=jnp.float32)
        if part == 0:
            result = result * HD ** (-0.5)
        qkv_ref[:, part * HW : (part + 1) * HW] = result.astype(jnp.bfloat16)


def block_start(owner, count, tokens):
    return jnp.minimum(owner * count, tokens - count)


def time_kernel(devices, frames, info, *refs):
    sources = refs[:devices]
    gain_ref, weight_ref = refs[devices : devices + 2]
    outs = refs[devices + 2 : 2 * devices + 2]
    normed_ref, qkv_ref, att_ref, bias_ref = refs[2 * devices + 2 :]
    half = devices * frames * 8
    group = frames * 8

    @pl.when(pl.program_id(0) == 0)
    def _():
        row = lax.broadcasted_iota(jnp.int32, (half, half), 0)
        col = lax.broadcasted_iota(jnp.int32, (half, half), 1)
        source = info[1] - col // group
        source = jnp.where(source < 0, source + devices, source)
        frame = source * frames + (col // 8) % frames
        valid = (row % 8 == col % 8) & (frame < info[2])
        bias_ref[...] = jnp.where(valid, 0.0, NEG).astype(jnp.float32)

    gain = gain_ref[...]
    for k, ref in enumerate(sources):
        values = ref[0] if k == 0 else ref[...]
        normed = values.astype(jnp.float32)
        for s in range(ROWS // 8):
            piece = normed[:, s * 8 : s * 8 + 8, :].reshape(group, normed.shape[-1])
            normed_ref[s * half + k * group : s * half + (k + 1) * group, :] = normalise(piece, gain)
    project_heads(normed_ref[...], weight_ref, qkv_ref)
    for s in range(ROWS // 8):
        attend(qkv_ref, pl.ds(s * half, half), bias_ref[...], att_ref)
    for k, ref in enumerate(outs):
        pieces = [
            att_ref[s * half + k * group : s * half + (k + 1) * group, :].astype(jnp.float32).reshape(frames, 8, HW)
            for s in range(ROWS // 8)
        ]
        ref[...] = jnp.concatenate(pieces, axis=1).astype(jnp.bfloat16)


def time_step(info, tokens, received, gain, weight, count):
    _, frames, _, width = tokens.shape
    devices = len(received) + 1
    rows = devices * frames * ROWS
    half = devices * frames * 8
    piece = pl.BlockSpec((frames, ROWS, width), lambda i, info: (0, i, 0))
    own = pl.BlockSpec((1, frames, ROWS, width), lambda i, info: (info[0], 0, info[3] + i, 0))
    whole = lambda a: pl.BlockSpec(a.shape, lambda i, info: (0,) * a.ndim)
    return pl.pallas_call(
        functools.partial(time_kernel, devices, frames),
        grid_spec=pltpu.PrefetchScalarGridSpec(
            num_scalar_prefetch=1,
            grid=(count // ROWS,),
            in_specs=[own] + [piece] * (devices - 1) + [whole(gain), whole(weight)],
            out_specs=[pl.BlockSpec((frames, ROWS, HW), lambda i, info: (0, i, 0))] * devices,
            scratch_shapes=[
                pltpu.VMEM((rows, width), jnp.bfloat16),
                pltpu.VMEM((rows, 3 * HW), jnp.bfloat16),
                pltpu.VMEM((rows, HW), jnp.bfloat16),
                pltpu.VMEM((half, half), jnp.float32),
            ],
        ),
        out_shape=[jax.ShapeDtypeStruct((frames, count, HW), jnp.bfloat16)] * devices,
        compiler_params=pltpu.CompilerParams(vmem_limit_bytes=VMEM_LIMIT),
        cost_estimate=pl.CostEstimate(
            flops=2 * count * devices * frames * width * 3 * HW, bytes_accessed=12_000_000, transcendentals=0
        ),
        name="time_attention",
    )(info, tokens, *received, gain, weight)


def space_kernel(devices, frames, count, aliased, info, x_ref, *refs):
    pieces = refs[:devices]
    time_out_ref, gain_ref, weight_ref, space_out_ref = refs[devices : devices + 4]
    refs = refs[devices + 4 + aliased :]
    out_ref, att_ref, mid_ref, qkv_ref = refs
    tokens = x_ref.shape[2]
    live = info[4] + info[5] + pl.program_id(0) < info[2]

    @pl.when(live)
    def _():
        for k, ref in enumerate(pieces):
            owner = info[1] + k
            owner = jnp.where(owner >= devices, owner - devices, owner)
            start = pl.multiple_of(block_start(owner, count, tokens), ROWS)
            att_ref[pl.ds(start, count), :] = ref[0]
        mid = x_ref[0, 0].astype(jnp.float32) + jnp.dot(
            att_ref[...], time_out_ref[...], preferred_element_type=jnp.float32
        )
        mid_ref[...] = mid.astype(jnp.bfloat16)
        project_heads(normalise(mid_ref[...].astype(jnp.float32), gain_ref[...]), weight_ref, qkv_ref)
        bias = jnp.where(lax.broadcasted_iota(jnp.int32, (1, tokens), 1) < info[3], 0.0, NEG).astype(jnp.float32)
        attend(qkv_ref, pl.ds(0, tokens), bias, att_ref)
        result = mid_ref[...].astype(jnp.float32) + jnp.dot(
            att_ref[...], space_out_ref[...], preferred_element_type=jnp.float32
        )
        keep = lax.broadcasted_iota(jnp.int32, (tokens, 1), 0) < info[3]
        out_ref[0, 0] = jnp.where(keep, result, 0.0).astype(jnp.bfloat16)

    @pl.when(jnp.logical_not(live))
    def _():
        out_ref[...] = jnp.zeros_like(out_ref)


def space_step(info, tokens, pieces, first, time_out, gain, weight, space_out, partial):
    _, _, places, width = tokens.shape
    devices = len(pieces)
    calls, count, _ = pieces[0].shape
    unit = pl.BlockSpec((1, 1, places, width), lambda i, info: (info[0], first + i, 0, 0))
    whole = lambda a: pl.BlockSpec(a.shape, lambda i, info: (0,) * a.ndim)
    aliased = partial is not None
    operands = [info, tokens, *pieces, time_out, gain, weight, space_out] + ([partial] if aliased else [])
    return pl.pallas_call(
        functools.partial(space_kernel, devices, calls, count, int(aliased)),
        grid_spec=pltpu.PrefetchScalarGridSpec(
            num_scalar_prefetch=1,
            grid=(calls,),
            in_specs=[unit]
            + [pl.BlockSpec((1, count, HW), lambda i, info: (i, 0, 0))] * devices
            + [whole(a) for a in (time_out, gain, weight, space_out)]
            + ([ANY] if aliased else []),
            out_specs=unit,
            scratch_shapes=[
                pltpu.VMEM((places, HW), jnp.bfloat16),
                pltpu.VMEM((places, width), jnp.bfloat16),
                pltpu.VMEM((places, 3 * HW), jnp.bfloat16),
            ],
        ),
        out_shape=jax.ShapeDtypeStruct(tokens.shape, jnp.bfloat16),
        input_output_aliases={len(operands) - 1: 0} if aliased else {},
        compiler_params=pltpu.CompilerParams(vmem_limit_bytes=VMEM_LIMIT),
        cost_estimate=pl.CostEstimate(
            flops=2 * calls * places * width * 5 * HW, bytes_accessed=8_000_000, transcendentals=0
        ),
        name="space_block",
    )(*operands)


def pack_kernel(devices, count, info, x_ref, *refs):
    outs = refs[: devices - 1]
    sems = refs[-1]
    tokens = x_ref.shape[2]
    copies = []
    for k, ref in enumerate(outs):
        owner = info[1] + k + 1
        owner = jnp.where(owner >= devices, owner - devices, owner)
        start = pl.multiple_of(block_start(owner, count, tokens), ROWS)
        copies.append(pltpu.make_async_copy(x_ref.at[info[0], :, pl.ds(start, count), :], ref, sems.at[k]))
    for copy in copies:
        copy.start()
    for copy in copies:
        copy.wait()


def pack_step(info, tokens, devices, count):
    _, frames, _, width = tokens.shape
    return pl.pallas_call(
        functools.partial(pack_kernel, devices, count),
        in_specs=[pl.BlockSpec(memory_space=pltpu.SMEM), ANY],
        out_specs=[ANY] * (devices - 1),
        out_shape=[jax.ShapeDtypeStruct((frames, count, width), jnp.bfloat16)] * (devices - 1),
        scratch_shapes=[pltpu.SemaphoreType.DMA((devices - 1,))],
        name="pack_tokens",
    )(info, tokens)


def after(values, done):
    return lax.optimization_barrier((tuple(values), tuple(done)))


def send(blocks, devices, forward):
    results = []
    for k, block in enumerate(blocks, 1):
        pairs = [(i, (i + k) % devices) if forward else ((i + k) % devices, i) for i in range(devices)]
        results.append(lax.ppermute(block, "frame", pairs))
    return results


def per_device(
    devices,
    video_tokens,
    frame_count,
    token_count,
    time_gain,
    time_qkv,
    time_out,
    space_gain,
    space_qkv,
    space_out,
):
    clips, frames, places, width = video_tokens.shape
    count = places // devices
    me = lax.axis_index("frame").astype(jnp.int32)
    time_gain = time_gain[None, :]
    space_gain = space_gain[None, :]
    first_frame = me * frames
    start = block_start(me, count, places) // ROWS

    def time_info(c):
        return jnp.stack([jnp.int32(c), me, frame_count[c], start])

    def space_info(c, first):
        return jnp.stack([jnp.int32(c), me, frame_count[c], token_count[c], first_frame, jnp.int32(first)])

    sent_a = pack_step(time_info(0), video_tokens, devices, count)
    got_a = send(sent_a, devices, True)
    sent_b = pack_step(time_info(1), video_tokens, devices, count)
    got_b = []
    for k in range(devices - 1):
        (block,), (got_a[k],) = after([sent_b[k]], [got_a[k]])
        pairs = [(i, (i + k + 1) % devices) for i in range(devices)]
        got_b.append(lax.ppermute(block, "frame", pairs))
    att_a = time_step(time_info(0), video_tokens, got_a, time_gain, time_qkv, count)
    back_a = [att_a[0]]
    for k in range(devices - 1):
        (block,), (got_b[k],) = after([att_a[k + 1]], [got_b[k]])
        pairs = [((i + k + 1) % devices, i) for i in range(devices)]
        back_a.append(lax.ppermute(block, "frame", pairs))
    att_b = time_step(time_info(1), video_tokens, got_b, time_gain, time_qkv, count)
    halves = [(0, frames // 2), (frames // 2, frames)]
    back_b = []
    for first, last in halves:
        blocks = [a[first:last] for a in att_b]
        back_b.append([blocks[0]] + send(blocks[1:], devices, False))
    weights = (time_out, space_gain, space_qkv, space_out)
    out = space_step(space_info(0, 0), video_tokens, back_a, 0, *weights, None)
    for (first, _), pieces in zip(halves, back_b):
        out = space_step(space_info(1, first), video_tokens, pieces, first, *weights, out)
    return out


def solution(mesh):
    placed = (P("clip", "frame", None, None), P("clip"), P("clip"), P(), P(), P(), P(), P(), P())
    return jax.shard_map(
        functools.partial(per_device, mesh.shape["frame"]),
        mesh=mesh,
        in_specs=placed,
        out_specs=P("clip", "frame", None, None),
        check_vma=False,
    )
```

```python
import functools

import jax
import jax.numpy as jnp
from jax import lax
from jax.experimental import pallas as pl
from jax.experimental.pallas import tpu as pltpu
from jax.sharding import PartitionSpec as P

HEADS = 8
HD = 64
HW = 512
ROWS = 16
NEG = -1e30
AHEAD = 0
BEHIND = 0
VMEM_LIMIT = 50 * 1024 * 1024
def KEPT(a):
    return pl.BlockSpec(a.shape, lambda i, *_: (0,) * a.ndim)


ANY = pl.BlockSpec(memory_space=pl.ANY)


def normalise(values, gain):
    centre = values - jnp.mean(values, axis=-1, keepdims=True)
    spread = jnp.mean(centre * centre, axis=-1, keepdims=True)
    return (centre * lax.rsqrt(spread + 1e-05) * gain).astype(jnp.bfloat16)


def attend(qkv_ref, rows, bias, out_ref):
    count = rows.size
    low = lax.broadcasted_iota(jnp.int32, (count, 2 * HD), 1) < HD
    zero = jnp.zeros((count, 2 * HD), jnp.bfloat16)
    for pair in range(HEADS // 2):
        cols = pair * 2 * HD
        q = qkv_ref[rows, cols : cols + 2 * HD]
        k = qkv_ref[rows, HW + cols : HW + cols + 2 * HD]
        v = qkv_ref[rows, 2 * HW + cols : 2 * HW + cols + 2 * HD]
        parts = []
        for keys in (jnp.where(low, k, zero), jnp.where(low, zero, k)):
            scores = lax.dot_general(q, keys, (((1,), (1,)), ((), ())), preferred_element_type=jnp.float32)
            scores = scores + bias
            expo = jnp.exp(scores - jnp.max(scores, axis=-1, keepdims=True))
            weights = (expo * (1.0 / jnp.sum(expo, axis=-1, keepdims=True))).astype(jnp.bfloat16)
            parts.append(jnp.dot(weights, v, preferred_element_type=jnp.float32))
        out_ref[rows, cols : cols + 2 * HD] = jnp.where(low, parts[0], parts[1]).astype(jnp.bfloat16)


def project_heads(normed, weight_ref, qkv_ref):
    for part in range(3):
        result = jnp.dot(normed, weight_ref[:, part * HW : (part + 1) * HW], preferred_element_type=jnp.float32)
        if part == 0:
            result = result * HD ** (-0.5)
        qkv_ref[:, part * HW : (part + 1) * HW] = result.astype(jnp.bfloat16)


def clip_at(slot, frame_count):
    return jnp.where(frame_count[1] > frame_count[0], 1 - slot, slot)


def block_start(owner, count, tokens):
    return jnp.minimum(owner * count, tokens - count)


class Route:
    def __init__(self, whole, devices, count):
        self.whole, self.devices, self.count = whole, devices, count

    def peer(self, me, k):
        return k if self.whole else me ^ k


def time_kernel(route, frames, slot, frame_count, *refs):
    devices = route.devices
    n_in = 1 if route.whole else devices
    sources = refs[:n_in]
    gain_ref, weight_ref = refs[n_in : n_in + 2]
    outs = refs[n_in + 2 : -4]
    normed_ref, qkv_ref, att_ref, bias_ref = refs[-4:]
    half = devices * frames * 8
    group = frames * 8
    me = lax.axis_index("frame")

    @pl.when(pl.program_id(0) == 0)
    def _():
        row = lax.broadcasted_iota(jnp.int32, (half, half), 0)
        col = lax.broadcasted_iota(jnp.int32, (half, half), 1)
        frame = route.peer(me, col // group) * frames + (col // 8) % frames
        valid = (row % 8 == col % 8) & (frame < frame_count[clip_at(slot, frame_count)])
        bias_ref[...] = jnp.where(valid, 0.0, NEG).astype(jnp.float32)

    gain = gain_ref[...]
    for k in range(devices):
        if route.whole:
            values = sources[0][k]
        else:
            values = sources[0][0] if k == 0 else sources[k][...]
        normed = values.astype(jnp.float32)
        for s in range(ROWS // 8):
            piece = normed[:, s * 8 : s * 8 + 8, :].reshape(group, normed.shape[-1])
            normed_ref[s * half + k * group : s * half + (k + 1) * group, :] = normalise(piece, gain)
    project_heads(normed_ref[...], weight_ref, qkv_ref)
    for s in range(ROWS // 8):
        attend(qkv_ref, pl.ds(s * half, half), bias_ref[...], att_ref)
    for k in range(devices):
        pieces = [
            att_ref[s * half + k * group : s * half + (k + 1) * group, :].astype(jnp.float32).reshape(frames, 8, HW)
            for s in range(ROWS // 8)
        ]
        result = jnp.concatenate(pieces, axis=1).astype(jnp.bfloat16)
        if route.whole:
            outs[0][k] = result
        else:
            early = outs[k].shape[0]
            outs[k][...] = result[:early]
            outs[-1][route.peer(me, k)] = result[early:]


def time_step(route, slot, frame_count, tokens, received, gain, weight, early=0):
    _, frames, places, width = tokens.shape
    devices, count = route.devices, route.count
    rows = devices * frames * ROWS
    half = devices * frames * 8

    def own_block(i, counts):
        start = block_start(lax.axis_index("frame"), count, places)
        return clip_at(slot, counts), 0, start // ROWS + i, 0

    if route.whole:
        operands = [received]
        in_specs = [pl.BlockSpec((devices, frames, ROWS, width), lambda i, *_: (0, 0, i, 0))]
        out_specs = [pl.BlockSpec((devices, frames, ROWS, HW), lambda i, *_: (0, 0, i, 0))]
        out_shape = [jax.ShapeDtypeStruct((devices, frames, count, HW), jnp.bfloat16)]
    else:
        operands = [tokens, *received]
        in_specs = [pl.BlockSpec((1, frames, ROWS, width), own_block)]
        in_specs += [pl.BlockSpec((frames, ROWS, width), lambda i, *_: (0, i, 0))] * (devices - 1)
        late = frames - early
        out_specs = [pl.BlockSpec((early, ROWS, HW), lambda i, *_: (0, i, 0))] * devices
        out_specs += [pl.BlockSpec((devices, late, ROWS, HW), lambda i, *_: (0, 0, i, 0))]
        out_shape = [jax.ShapeDtypeStruct((early, count, HW), jnp.bfloat16)] * devices
        out_shape += [jax.ShapeDtypeStruct((devices, late, count, HW), jnp.bfloat16)]
    return pl.pallas_call(
        functools.partial(time_kernel, route, frames, slot),
        grid_spec=pltpu.PrefetchScalarGridSpec(
            num_scalar_prefetch=1,
            grid=(count // ROWS,),
            in_specs=in_specs + [KEPT(gain), KEPT(weight)],
            out_specs=out_specs,
            scratch_shapes=[
                pltpu.VMEM((rows, width), jnp.bfloat16),
                pltpu.VMEM((rows, 3 * HW), jnp.bfloat16),
                pltpu.VMEM((rows, HW), jnp.bfloat16),
                pltpu.VMEM((half, half), jnp.float32),
            ],
        ),
        out_shape=out_shape,
        compiler_params=pltpu.CompilerParams(vmem_limit_bytes=VMEM_LIMIT),
        cost_estimate=pl.CostEstimate(
            flops=4 * count * devices * frames * width * 3 * HW, bytes_accessed=12_000_000, transcendentals=0
        ),
        name="time_attention",
    )(frame_count, *operands, gain, weight)


def space_kernel(route, frames, slot, first, aliased, frame_count, token_count, x_ref, *refs):
    devices, count = route.devices, route.count
    n_in = 1 if route.whole else devices
    pieces = refs[:n_in]
    gain_ref, time_out_ref, weight_ref, space_out_ref = refs[n_in : n_in + 4]
    out_ref, att_ref, mid_ref, qkv_ref = refs[n_in + 4 + aliased :]
    tokens = x_ref.shape[2]
    me = lax.axis_index("frame")
    clip = clip_at(slot, frame_count)
    token_end = token_count[clip]
    live = me * frames + first + pl.program_id(0) < frame_count[clip]

    @pl.when(live)
    def _():
        for k in range(devices):
            start = pl.multiple_of(block_start(route.peer(me, k), count, tokens), ROWS)
            att_ref[pl.ds(start, count), :] = pieces[0][k, 0] if route.whole else pieces[k][0]
        mid = x_ref[0, 0].astype(jnp.float32) + jnp.dot(
            att_ref[...], time_out_ref[...], preferred_element_type=jnp.float32
        )
        mid_ref[...] = mid.astype(jnp.bfloat16)
        normed = normalise(mid_ref[...].astype(jnp.float32), gain_ref[...])
        project_heads(normed, weight_ref, qkv_ref)
        bias = jnp.where(lax.broadcasted_iota(jnp.int32, (1, tokens), 1) < token_end, 0.0, NEG).astype(jnp.float32)
        attend(qkv_ref, pl.ds(0, tokens), bias, att_ref)
        result = mid_ref[...].astype(jnp.float32) + jnp.dot(
            att_ref[...], space_out_ref[...], preferred_element_type=jnp.float32
        )
        keep = lax.broadcasted_iota(jnp.int32, (tokens, 1), 0) < token_end
        out_ref[0, 0] = jnp.where(keep, result, 0.0).astype(jnp.bfloat16)

    @pl.when(jnp.logical_not(live))
    def _():
        out_ref[...] = jnp.zeros_like(out_ref)


def space_step(route, slot, counts, tokens, pieces, offset, first, calls, weights, partial):
    _, frames, places, width = tokens.shape
    devices, count = route.devices, route.count
    skip = first - offset
    unit = pl.BlockSpec((1, 1, places, width), lambda i, c, t: (clip_at(slot, c), first + i, 0, 0))
    if route.whole:
        piece_specs = [pl.BlockSpec((devices, 1, count, HW), lambda i, *_: (0, skip + i, 0, 0))]
    else:
        piece_specs = [pl.BlockSpec((1, count, HW), lambda i, *_: (skip + i, 0, 0))] * devices
    aliased = partial is not None
    operands = [*counts, tokens, *pieces, *weights] + ([partial] if aliased else [])
    return pl.pallas_call(
        functools.partial(space_kernel, route, frames, slot, first, int(aliased)),
        grid_spec=pltpu.PrefetchScalarGridSpec(
            num_scalar_prefetch=2,
            grid=(calls,),
            in_specs=[unit] + piece_specs + [KEPT(a) for a in weights] + ([ANY] if aliased else []),
            out_specs=unit,
            scratch_shapes=[
                pltpu.VMEM((places, HW), jnp.bfloat16),
                pltpu.VMEM((places, width), jnp.bfloat16),
                pltpu.VMEM((places, 3 * HW), jnp.bfloat16),
            ],
        ),
        out_shape=jax.ShapeDtypeStruct(tokens.shape, jnp.bfloat16),
        input_output_aliases={len(operands) - 1: 0} if aliased else {},
        compiler_params=pltpu.CompilerParams(vmem_limit_bytes=VMEM_LIMIT),
        cost_estimate=pl.CostEstimate(
            flops=4 * calls * places * width * 5 * HW, bytes_accessed=8_000_000, transcendentals=0
        ),
        name="space_block",
    )(*operands)


def pack_kernel(route, slot, counts, x_ref, *refs):
    outs = refs[:-3]
    held, in_sems, out_sems = refs[-3:]
    devices, count = route.devices, route.count
    first = 0 if route.whole else 1
    clip = clip_at(slot, counts)
    loads, stores = [], []
    for k in range(first, devices):
        start = pl.multiple_of(block_start(route.peer(lax.axis_index("frame"), k), count, x_ref.shape[2]), ROWS)
        loads.append(pltpu.make_async_copy(x_ref.at[clip, :, pl.ds(start, count), :], held.at[k], in_sems.at[k]))
        target = outs[0].at[k] if route.whole else outs[k - first]
        stores.append(pltpu.make_async_copy(held.at[k], target, out_sems.at[k]))
    for load in loads:
        load.start()
    for load, store in zip(loads, stores):
        load.wait()
        store.start()
    for store in stores:
        store.wait()


def pack_step(route, slot, frame_count, tokens):
    _, frames, _, width = tokens.shape
    devices, count = route.devices, route.count
    if route.whole:
        out_shape = [jax.ShapeDtypeStruct((devices, frames, count, width), jnp.bfloat16)]
    else:
        out_shape = [jax.ShapeDtypeStruct((frames, count, width), jnp.bfloat16)] * (devices - 1)
    return pl.pallas_call(
        functools.partial(pack_kernel, route, slot),
        in_specs=[pl.BlockSpec(memory_space=pltpu.SMEM), ANY],
        out_specs=[ANY] * len(out_shape),
        out_shape=out_shape,
        scratch_shapes=[
            pltpu.VMEM((devices, frames, count, width), jnp.bfloat16),
            pltpu.SemaphoreType.DMA((devices,)),
            pltpu.SemaphoreType.DMA((devices,)),
        ],
        compiler_params=pltpu.CompilerParams(vmem_limit_bytes=VMEM_LIMIT),
        name="pack_tokens",
    )(frame_count, tokens)


def exchange_all(block):
    return lax.all_to_all(block, "frame", 0, 0, tiled=True)


def exchange(block, devices, k):
    return lax.ppermute(block, "frame", [(i, i ^ k) for i in range(devices)])


def far_and_near(devices):
    half = devices // 2
    order = []
    for k in range(half):
        order += [half + k, k + 1]
    return order[: devices - 1]


def per_device(
    devices,
    video_tokens,
    frame_count,
    token_count,
    time_gain,
    time_qkv,
    time_out,
    space_gain,
    space_qkv,
    space_out,
):
    _, frames, places, _ = video_tokens.shape
    time_weights = (time_gain[None, :], time_qkv)
    space_weights = (space_gain[None, :], time_out, space_qkv, space_out)
    counts = (frame_count, token_count)
    half = frames // 2
    one = Route(True, devices, places // devices)
    two = Route(False, devices, places // devices)
    order = far_and_near(devices)

    (sent_a,) = pack_step(one, 0, frame_count, video_tokens)
    got_a = exchange_all(sent_a)
    sent_b = pack_step(two, 1, frame_count, video_tokens)
    got_b = {}
    for place, k in enumerate(order):
        if place == AHEAD:
            sent_b, got_a = lax.optimization_barrier((sent_b, got_a))
        got_b[k] = exchange(sent_b[k - 1], devices, k)
    (att_a,) = time_step(one, 0, frame_count, video_tokens, got_a, *time_weights)
    for k in order[: len(order) - BEHIND]:
        att_a, got_b[k] = lax.optimization_barrier((att_a, got_b[k]))
    back_a = exchange_all(att_a)
    received = [got_b[k] for k in range(1, devices)]
    *early_b, late_b = time_step(two, 1, frame_count, video_tokens, received, *time_weights, early=half)
    back_b = {k: exchange(early_b[k], devices, k) for k in order}
    late_b = exchange_all(late_b)
    back_b = [early_b[0]] + [back_b[k] for k in range(1, devices)]
    out = space_step(one, 0, counts, video_tokens, [back_a], 0, 0, frames, space_weights, None)
    out = space_step(two, 1, counts, video_tokens, back_b, 0, 0, half, space_weights, out)
    return space_step(one, 1, counts, video_tokens, [late_b], half, half, frames - half, space_weights, out)


def solution(mesh):
    placed = (P("clip", "frame", None, None), P("clip"), P("clip"), P(), P(), P(), P(), P(), P())
    return jax.shard_map(
        functools.partial(per_device, mesh.shape["frame"]),
        mesh=mesh,
        in_specs=placed,
        out_specs=P("clip", "frame", None, None),
        check_vma=False,
    )
```

```python
import functools

import jax
import jax.numpy as jnp
from jax import lax
from jax.experimental import pallas as pl
from jax.experimental.pallas import tpu as pltpu
from jax.sharding import PartitionSpec as P

HEADS = 8
HD = 64
HW = 512
ROWS = 16
NEG = -1e30
LEAD = 2
TAIL = 7
VMEM_LIMIT = 56 * 1024 * 1024
def KEPT(a):
    return pl.BlockSpec(a.shape, lambda i, *_: (0,) * a.ndim)


ANY = pl.BlockSpec(memory_space=pl.ANY)


def normalise(values, gain):
    centre = values - jnp.mean(values, axis=-1, keepdims=True)
    spread = jnp.mean(centre * centre, axis=-1, keepdims=True)
    return (centre * lax.rsqrt(spread + 1e-05) * gain).astype(jnp.bfloat16)


def attend(qkv_ref, rows, bias, out_ref):
    count = rows.size
    low = lax.broadcasted_iota(jnp.int32, (count, 2 * HD), 1) < HD
    zero = jnp.zeros((count, 2 * HD), jnp.bfloat16)
    for pair in range(HEADS // 2):
        cols = pair * 2 * HD
        q = qkv_ref[rows, cols : cols + 2 * HD]
        k = qkv_ref[rows, HW + cols : HW + cols + 2 * HD]
        v = qkv_ref[rows, 2 * HW + cols : 2 * HW + cols + 2 * HD]
        parts = []
        for keys in (jnp.where(low, k, zero), jnp.where(low, zero, k)):
            scores = lax.dot_general(q, keys, (((1,), (1,)), ((), ())), preferred_element_type=jnp.float32)
            scores = scores + bias
            expo = jnp.exp(scores - jnp.max(scores, axis=-1, keepdims=True))
            weights = (expo * (1.0 / jnp.sum(expo, axis=-1, keepdims=True))).astype(jnp.bfloat16)
            parts.append(jnp.dot(weights, v, preferred_element_type=jnp.float32))
        out_ref[rows, cols : cols + 2 * HD] = jnp.where(low, parts[0], parts[1]).astype(jnp.bfloat16)


def project_heads(normed, weight_ref, qkv_ref):
    for part in range(3):
        result = jnp.dot(normed, weight_ref[:, part * HW : (part + 1) * HW], preferred_element_type=jnp.float32)
        if part == 0:
            result = result * HD ** (-0.5)
        qkv_ref[:, part * HW : (part + 1) * HW] = result.astype(jnp.bfloat16)


def clip_at(slot, frame_count):
    return jnp.where(frame_count[1] > frame_count[0], 1 - slot, slot)


def block_start(owner, count, tokens):
    return jnp.minimum(owner * count, tokens - count)


class Route:
    def __init__(self, whole, devices, count):
        self.whole, self.devices, self.count = whole, devices, count

    def peer(self, me, k):
        return k if self.whole else me ^ k


def time_kernel(route, back, frames, slot, frame_count, *refs):
    devices = route.devices
    n_in = 1 if route.whole else devices
    sources = refs[:n_in]
    gain_ref, weight_ref = refs[n_in : n_in + 2]
    outs = refs[n_in + 2 : -4]
    normed_ref, qkv_ref, att_ref, bias_ref = refs[-4:]
    half = devices * frames * 8
    group = frames * 8
    me = lax.axis_index("frame")

    @pl.when(pl.program_id(0) == 0)
    def _():
        row = lax.broadcasted_iota(jnp.int32, (half, half), 0)
        col = lax.broadcasted_iota(jnp.int32, (half, half), 1)
        frame = (back if route.whole else route).peer(me, col // group) * frames + (col // 8) % frames
        valid = (row % 8 == col % 8) & (frame < frame_count[clip_at(slot, frame_count)])
        bias_ref[...] = jnp.where(valid, 0.0, NEG).astype(jnp.float32)

    gain = gain_ref[...]
    for k in range(devices):
        if route.whole:
            values = sources[0][back.peer(me, k)]
        else:
            values = sources[0][0] if k == 0 else sources[k][...]
        normed = values.astype(jnp.float32)
        for s in range(ROWS // 8):
            piece = normed[:, s * 8 : s * 8 + 8, :].reshape(group, normed.shape[-1])
            normed_ref[s * half + k * group : s * half + (k + 1) * group, :] = normalise(piece, gain)
    project_heads(normed_ref[...], weight_ref, qkv_ref)
    for s in range(ROWS // 8):
        attend(qkv_ref, pl.ds(s * half, half), bias_ref[...], att_ref)
    for k in range(devices):
        pieces = [
            att_ref[s * half + k * group : s * half + (k + 1) * group, :].astype(jnp.float32).reshape(frames, 8, HW)
            for s in range(ROWS // 8)
        ]
        result = jnp.concatenate(pieces, axis=1).astype(jnp.bfloat16)
        if back.whole:
            outs[0][route.peer(me, k)] = result
        else:
            outs[k][...] = result


def time_step(route, back, slot, frame_count, tokens, received, gain, weight):
    _, frames, places, width = tokens.shape
    devices, count = route.devices, route.count
    rows = devices * frames * ROWS
    half = devices * frames * 8

    def own_block(i, counts):
        start = block_start(lax.axis_index("frame"), count, places)
        return clip_at(slot, counts), 0, start // ROWS + i, 0

    if route.whole:
        operands = [received]
        in_specs = [pl.BlockSpec((devices, frames, ROWS, width), lambda i, *_: (0, 0, i, 0))]
    else:
        operands = [tokens, *received]
        in_specs = [pl.BlockSpec((1, frames, ROWS, width), own_block)]
        in_specs += [pl.BlockSpec((frames, ROWS, width), lambda i, *_: (0, i, 0))] * (devices - 1)
    if back.whole:
        out_specs = [pl.BlockSpec((devices, frames, ROWS, HW), lambda i, *_: (0, 0, i, 0))]
        out_shape = [jax.ShapeDtypeStruct((devices, frames, count, HW), jnp.bfloat16)]
    else:
        out_specs = [pl.BlockSpec((frames, ROWS, HW), lambda i, *_: (0, i, 0))] * devices
        out_shape = [jax.ShapeDtypeStruct((frames, count, HW), jnp.bfloat16)] * devices
    return pl.pallas_call(
        functools.partial(time_kernel, route, back, frames, slot),
        grid_spec=pltpu.PrefetchScalarGridSpec(
            num_scalar_prefetch=1,
            grid=(count // ROWS,),
            in_specs=in_specs + [KEPT(gain), KEPT(weight)],
            out_specs=out_specs,
            scratch_shapes=[
                pltpu.VMEM((rows, width), jnp.bfloat16),
                pltpu.VMEM((rows, 3 * HW), jnp.bfloat16),
                pltpu.VMEM((rows, HW), jnp.bfloat16),
                pltpu.VMEM((half, half), jnp.float32),
            ],
        ),
        out_shape=out_shape,
        compiler_params=pltpu.CompilerParams(vmem_limit_bytes=VMEM_LIMIT),
        cost_estimate=pl.CostEstimate(
            flops=4 * count * devices * frames * width * 3 * HW, bytes_accessed=12_000_000, transcendentals=0
        ),
        name="time_attention",
    )(frame_count, *operands, gain, weight)


def space_kernel(route, frames, slot, first, aliased, frame_count, token_count, x_ref, *refs):
    devices, count = route.devices, route.count
    n_in = 1 if route.whole else devices
    pieces = refs[:n_in]
    gain_ref, time_out_ref, weight_ref, space_out_ref = refs[n_in : n_in + 4]
    out_ref, att_ref, mid_ref, qkv_ref = refs[n_in + 4 + aliased :]
    tokens = x_ref.shape[2]
    me = lax.axis_index("frame")
    clip = clip_at(slot, frame_count)
    token_end = token_count[clip]
    live = me * frames + first + pl.program_id(0) < frame_count[clip]

    @pl.when(live)
    def _():
        for k in range(devices):
            start = pl.multiple_of(block_start(route.peer(me, k), count, tokens), ROWS)
            att_ref[pl.ds(start, count), :] = pieces[0][k, 0] if route.whole else pieces[k][0]
        mid = x_ref[0, 0].astype(jnp.float32) + jnp.dot(
            att_ref[...], time_out_ref[...], preferred_element_type=jnp.float32
        )
        mid_ref[...] = mid.astype(jnp.bfloat16)
        normed = normalise(mid_ref[...].astype(jnp.float32), gain_ref[...])
        project_heads(normed, weight_ref, qkv_ref)
        bias = jnp.where(lax.broadcasted_iota(jnp.int32, (1, tokens), 1) < token_end, 0.0, NEG).astype(jnp.float32)
        attend(qkv_ref, pl.ds(0, tokens), bias, att_ref)
        result = mid_ref[...].astype(jnp.float32) + jnp.dot(
            att_ref[...], space_out_ref[...], preferred_element_type=jnp.float32
        )
        keep = lax.broadcasted_iota(jnp.int32, (tokens, 1), 0) < token_end
        out_ref[0, 0] = jnp.where(keep, result, 0.0).astype(jnp.bfloat16)

    @pl.when(jnp.logical_not(live))
    def _():
        out_ref[...] = jnp.zeros_like(out_ref)


def space_step(route, slot, counts, tokens, pieces, offset, first, calls, weights, partial):
    _, frames, places, width = tokens.shape
    devices, count = route.devices, route.count
    skip = first - offset
    unit = pl.BlockSpec((1, 1, places, width), lambda i, c, t: (clip_at(slot, c), first + i, 0, 0))
    if route.whole:
        piece_specs = [pl.BlockSpec((devices, 1, count, HW), lambda i, *_: (0, skip + i, 0, 0))]
    else:
        piece_specs = [pl.BlockSpec((1, count, HW), lambda i, *_: (skip + i, 0, 0))] * devices
    aliased = partial is not None
    operands = [*counts, tokens, *pieces, *weights] + ([partial] if aliased else [])
    return pl.pallas_call(
        functools.partial(space_kernel, route, frames, slot, first, int(aliased)),
        grid_spec=pltpu.PrefetchScalarGridSpec(
            num_scalar_prefetch=2,
            grid=(calls,),
            in_specs=[unit] + piece_specs + [KEPT(a) for a in weights] + ([ANY] if aliased else []),
            out_specs=unit,
            scratch_shapes=[
                pltpu.VMEM((places, HW), jnp.bfloat16),
                pltpu.VMEM((places, width), jnp.bfloat16),
                pltpu.VMEM((places, 3 * HW), jnp.bfloat16),
            ],
        ),
        out_shape=jax.ShapeDtypeStruct(tokens.shape, jnp.bfloat16),
        input_output_aliases={len(operands) - 1: 0} if aliased else {},
        compiler_params=pltpu.CompilerParams(vmem_limit_bytes=VMEM_LIMIT),
        cost_estimate=pl.CostEstimate(
            flops=4 * calls * places * width * 5 * HW, bytes_accessed=8_000_000, transcendentals=0
        ),
        name="space_block",
    )(*operands)


def pack_kernel(route, slot, counts, x_ref, *refs):
    outs = refs[:-3]
    held, in_sems, out_sems = refs[-3:]
    devices, count = route.devices, route.count
    first = 0 if route.whole else 1
    clip = clip_at(slot, counts)
    loads, stores = [], []
    for k in range(first, devices):
        start = pl.multiple_of(block_start(route.peer(lax.axis_index("frame"), k), count, x_ref.shape[2]), ROWS)
        loads.append(pltpu.make_async_copy(x_ref.at[clip, :, pl.ds(start, count), :], held.at[k], in_sems.at[k]))
        target = outs[0].at[k] if route.whole else outs[k - first]
        stores.append(pltpu.make_async_copy(held.at[k], target, out_sems.at[k]))
    for load in loads:
        load.start()
    for load, store in zip(loads, stores):
        load.wait()
        store.start()
    for store in stores:
        store.wait()


def pack_step(route, slot, frame_count, tokens):
    _, frames, _, width = tokens.shape
    devices, count = route.devices, route.count
    if route.whole:
        out_shape = [jax.ShapeDtypeStruct((devices, frames, count, width), jnp.bfloat16)]
    else:
        out_shape = [jax.ShapeDtypeStruct((frames, count, width), jnp.bfloat16)] * (devices - 1)
    return pl.pallas_call(
        functools.partial(pack_kernel, route, slot),
        in_specs=[pl.BlockSpec(memory_space=pltpu.SMEM), ANY],
        out_specs=[ANY] * len(out_shape),
        out_shape=out_shape,
        scratch_shapes=[
            pltpu.VMEM((devices, frames, count, width), jnp.bfloat16),
            pltpu.SemaphoreType.DMA((devices,)),
            pltpu.SemaphoreType.DMA((devices,)),
        ],
        compiler_params=pltpu.CompilerParams(vmem_limit_bytes=VMEM_LIMIT),
        name="pack_tokens",
    )(frame_count, tokens)


def exchange_all(block):
    return lax.all_to_all(block, "frame", 0, 0, tiled=True)


def exchange(block, devices, k):
    return lax.ppermute(block, "frame", [(i, i ^ k) for i in range(devices)])


def far_and_near(devices):
    half = devices // 2
    order = []
    for k in range(half):
        order += [half + k, k + 1]
    return order[: devices - 1]


def per_device(
    devices,
    video_tokens,
    frame_count,
    token_count,
    time_gain,
    time_qkv,
    time_out,
    space_gain,
    space_qkv,
    space_out,
):
    _, frames, places, _ = video_tokens.shape
    time_weights = (time_gain[None, :], time_qkv)
    space_weights = (space_gain[None, :], time_out, space_qkv, space_out)
    counts = (frame_count, token_count)
    one = Route(True, devices, places // devices)
    two = Route(False, devices, places // devices)
    order = far_and_near(devices)

    (sent_a,) = pack_step(one, 0, frame_count, video_tokens)
    got_a = exchange_all(sent_a)
    sent_b = pack_step(two, 1, frame_count, video_tokens)
    sent_b, _ = lax.optimization_barrier((sent_b, got_a))
    got_b = {k: exchange(sent_b[k - 1], devices, k) for k in order}
    att_a = time_step(one, two, 0, frame_count, video_tokens, got_a, *time_weights)
    earlier = [got_b[k] for k in order]
    back_a = {}
    for place, k in enumerate(order):
        block, _ = lax.optimization_barrier((att_a[k], earlier[: place + LEAD]))
        back_a[k] = exchange(block, devices, k)
        earlier.append(back_a[k])
    received = [got_b[k] for k in range(1, devices)]
    (att_b,) = time_step(two, one, 1, frame_count, video_tokens, received, *time_weights)
    att_b, _ = lax.optimization_barrier((att_b, earlier[: len(order) + TAIL]))
    back_b = exchange_all(att_b)
    back_a = [att_a[0]] + [back_a[k] for k in range(1, devices)]
    out = space_step(two, 0, counts, video_tokens, back_a, 0, 0, frames, space_weights, None)
    return space_step(one, 1, counts, video_tokens, [back_b], 0, 0, frames, space_weights, out)


def solution(mesh):
    placed = (P("clip", "frame", None, None), P("clip"), P("clip"), P(), P(), P(), P(), P(), P())
    return jax.shard_map(
        functools.partial(per_device, mesh.shape["frame"]),
        mesh=mesh,
        in_specs=placed,
        out_specs=P("clip", "frame", None, None),
        check_vma=False,
    )
```

```python
import functools

import jax
import jax.numpy as jnp
from jax import lax
from jax.experimental import pallas as pl
from jax.experimental.pallas import tpu as pltpu
from jax.sharding import PartitionSpec as P

HEADS = 8
HD = 64
HW = 512
ROWS = 16
NEG = -1e30
PER = 2
LEAD = 2
TAIL = 7
VMEM_LIMIT = 56 * 1024 * 1024
def KEPT(a):
    return pl.BlockSpec(a.shape, lambda i, *_: (0,) * a.ndim)


ANY = pl.BlockSpec(memory_space=pl.ANY)


def normalise(values, gain):
    centre = values - jnp.mean(values, axis=-1, keepdims=True)
    spread = jnp.mean(centre * centre, axis=-1, keepdims=True)
    return (centre * lax.rsqrt(spread + 1e-05) * gain).astype(jnp.bfloat16)


def attend(qkv_ref, rows, bias, out_ref):
    count = rows.size
    low = lax.broadcasted_iota(jnp.int32, (count, 2 * HD), 1) < HD
    zero = jnp.zeros((count, 2 * HD), jnp.bfloat16)
    scores = []
    for pair in range(HEADS // 2):
        cols = pair * 2 * HD
        q = qkv_ref[rows, cols : cols + 2 * HD]
        k = qkv_ref[rows, HW + cols : HW + cols + 2 * HD]
        for keys in (jnp.where(low, k, zero), jnp.where(low, zero, k)):
            scores.append(lax.dot_general(q, keys, (((1,), (1,)), ((), ())), preferred_element_type=jnp.float32))
    weights = []
    for score in scores:
        score = score + bias
        expo = jnp.exp(score - jnp.max(score, axis=-1, keepdims=True))
        weights.append((expo * (1.0 / jnp.sum(expo, axis=-1, keepdims=True))).astype(jnp.bfloat16))
    for pair in range(HEADS // 2):
        cols = pair * 2 * HD
        v = qkv_ref[rows, 2 * HW + cols : 2 * HW + cols + 2 * HD]
        parts = [jnp.dot(weights[2 * pair + j], v, preferred_element_type=jnp.float32) for j in range(2)]
        out_ref[rows, cols : cols + 2 * HD] = jnp.where(low, parts[0], parts[1]).astype(jnp.bfloat16)


def project_heads(normed, weight_ref, qkv_ref):
    for part in range(3):
        result = jnp.dot(normed, weight_ref[:, part * HW : (part + 1) * HW], preferred_element_type=jnp.float32)
        if part == 0:
            result = result * HD ** (-0.5)
        qkv_ref[:, part * HW : (part + 1) * HW] = result.astype(jnp.bfloat16)


def clip_at(slot, frame_count):
    return jnp.where(frame_count[1] > frame_count[0], 1 - slot, slot)


def block_start(owner, count, tokens):
    return jnp.minimum(owner * count, tokens - count)


class Route:
    def __init__(self, whole, devices, count):
        self.whole, self.devices, self.count = whole, devices, count

    def peer(self, me, k):
        return k if self.whole else me ^ k


def time_kernel(route, back, frames, slot, frame_count, *refs):
    devices = route.devices
    n_in = 1 if route.whole else devices
    sources = refs[:n_in]
    gain_ref, weight_ref = refs[n_in : n_in + 2]
    outs = refs[n_in + 2 : -4]
    normed_ref, qkv_ref, att_ref, bias_ref = refs[-4:]
    half = devices * frames * 8
    group = frames * 8
    me = lax.axis_index("frame")

    @pl.when(pl.program_id(0) == 0)
    def _():
        row = lax.broadcasted_iota(jnp.int32, (half, half), 0)
        col = lax.broadcasted_iota(jnp.int32, (half, half), 1)
        frame = (back if route.whole else route).peer(me, col // group) * frames + (col // 8) % frames
        valid = (row % 8 == col % 8) & (frame < frame_count[clip_at(slot, frame_count)])
        bias_ref[...] = jnp.where(valid, 0.0, NEG).astype(jnp.float32)

    gain = gain_ref[...]
    for k in range(devices):
        if route.whole:
            values = sources[0][back.peer(me, k)]
        else:
            values = sources[0][0] if k == 0 else sources[k][...]
        normed = values.astype(jnp.float32)
        for s in range(ROWS // 8):
            piece = normed[:, s * 8 : s * 8 + 8, :].reshape(group, normed.shape[-1])
            normed_ref[s * half + k * group : s * half + (k + 1) * group, :] = normalise(piece, gain)
    for s in range(ROWS // 8):
        rows = pl.ds(s * half, half)
        project_heads(normed_ref[rows, :], weight_ref, qkv_ref.at[rows])
    for s in range(ROWS // 8):
        attend(qkv_ref, pl.ds(s * half, half), bias_ref[...], att_ref)
    for k in range(devices):
        pieces = [
            att_ref[s * half + k * group : s * half + (k + 1) * group, :].astype(jnp.float32).reshape(frames, 8, HW)
            for s in range(ROWS // 8)
        ]
        result = jnp.concatenate(pieces, axis=1).astype(jnp.bfloat16)
        if back.whole:
            outs[0][route.peer(me, k)] = result
        else:
            outs[k][...] = result


def time_step(route, back, slot, frame_count, tokens, received, gain, weight):
    _, frames, places, width = tokens.shape
    devices, count = route.devices, route.count
    rows = devices * frames * ROWS
    half = devices * frames * 8

    def own_block(i, counts):
        start = block_start(lax.axis_index("frame"), count, places)
        return clip_at(slot, counts), 0, start // ROWS + i, 0

    if route.whole:
        operands = [received]
        in_specs = [pl.BlockSpec((devices, frames, ROWS, width), lambda i, *_: (0, 0, i, 0))]
    else:
        operands = [tokens, *received]
        in_specs = [pl.BlockSpec((1, frames, ROWS, width), own_block)]
        in_specs += [pl.BlockSpec((frames, ROWS, width), lambda i, *_: (0, i, 0))] * (devices - 1)
    if back.whole:
        out_specs = [pl.BlockSpec((devices, frames, ROWS, HW), lambda i, *_: (0, 0, i, 0))]
        out_shape = [jax.ShapeDtypeStruct((devices, frames, count, HW), jnp.bfloat16)]
    else:
        out_specs = [pl.BlockSpec((frames, ROWS, HW), lambda i, *_: (0, i, 0))] * devices
        out_shape = [jax.ShapeDtypeStruct((frames, count, HW), jnp.bfloat16)] * devices
    return pl.pallas_call(
        functools.partial(time_kernel, route, back, frames, slot),
        grid_spec=pltpu.PrefetchScalarGridSpec(
            num_scalar_prefetch=1,
            grid=(count // ROWS,),
            in_specs=in_specs + [KEPT(gain), KEPT(weight)],
            out_specs=out_specs,
            scratch_shapes=[
                pltpu.VMEM((rows, width), jnp.bfloat16),
                pltpu.VMEM((rows, 3 * HW), jnp.bfloat16),
                pltpu.VMEM((rows, HW), jnp.bfloat16),
                pltpu.VMEM((half, half), jnp.float32),
            ],
        ),
        out_shape=out_shape,
        compiler_params=pltpu.CompilerParams(vmem_limit_bytes=VMEM_LIMIT),
        cost_estimate=pl.CostEstimate(
            flops=4 * count * devices * frames * width * 3 * HW, bytes_accessed=12_000_000, transcendentals=0
        ),
        name="time_attention",
    )(frame_count, *operands, gain, weight)


def space_kernel(route, frames, slot, first, per, aliased, frame_count, token_count, x_ref, *refs):
    devices, count = route.devices, route.count
    n_in = 1 if route.whole else devices
    pieces = refs[:n_in]
    gain_ref, time_out_ref, weight_ref, space_out_ref = refs[n_in : n_in + 4]
    out_ref = refs[n_in + 4 + aliased]
    scratch = refs[n_in + 5 + aliased :]
    tokens = x_ref.shape[2]
    me = lax.axis_index("frame")
    clip = clip_at(slot, frame_count)
    token_end = token_count[clip]
    begin = me * frames + first + pl.program_id(0) * per
    live = begin < frame_count[clip]

    @pl.when(live)
    def _():
        bias = jnp.where(lax.broadcasted_iota(jnp.int32, (1, tokens), 1) < token_end, 0.0, NEG).astype(jnp.float32)
        place = lax.broadcasted_iota(jnp.int32, (tokens, 1), 0)
        att_ref, mid_ref, qkv_ref = scratch
        for f in range(per):
            for k in range(devices):
                start = pl.multiple_of(block_start(route.peer(me, k), count, tokens), ROWS) + f * tokens
                att_ref[pl.ds(start, count), :] = pieces[0][k, f] if route.whole else pieces[k][f]
        mid = x_ref[0].reshape(per * tokens, -1).astype(jnp.float32) + jnp.dot(
            att_ref[...], time_out_ref[...], preferred_element_type=jnp.float32
        )
        mid_ref[...] = mid.astype(jnp.bfloat16)
        for f in range(per):
            rows = pl.ds(f * tokens, tokens)
            project_heads(normalise(mid_ref[rows, :].astype(jnp.float32), gain_ref[...]), weight_ref, qkv_ref.at[rows])
        for f in range(per):
            attend(qkv_ref, pl.ds(f * tokens, tokens), bias, att_ref)
        result = mid_ref[...].astype(jnp.float32) + jnp.dot(
            att_ref[...], space_out_ref[...], preferred_element_type=jnp.float32
        )
        for f in range(per):
            keep = (place < token_end) & (begin + f < frame_count[clip])
            out_ref[0, f] = jnp.where(keep, result[f * tokens : (f + 1) * tokens], 0.0).astype(jnp.bfloat16)

    @pl.when(jnp.logical_not(live))
    def _():
        out_ref[...] = jnp.zeros_like(out_ref)


def space_step(route, slot, counts, tokens, pieces, offset, first, calls, weights, partial):
    _, frames, places, width = tokens.shape
    devices, count = route.devices, route.count
    per = PER if calls % PER == 0 and first % PER == 0 and offset % PER == 0 else 1
    skip = (first - offset) // per
    unit = pl.BlockSpec((1, per, places, width), lambda i, c, t: (clip_at(slot, c), first // per + i, 0, 0))
    if route.whole:
        piece_specs = [pl.BlockSpec((devices, per, count, HW), lambda i, *_: (0, skip + i, 0, 0))]
    else:
        piece_specs = [pl.BlockSpec((per, count, HW), lambda i, *_: (skip + i, 0, 0))] * devices
    aliased = partial is not None
    operands = [*counts, tokens, *pieces, *weights] + ([partial] if aliased else [])
    return pl.pallas_call(
        functools.partial(space_kernel, route, frames, slot, first, per, int(aliased)),
        grid_spec=pltpu.PrefetchScalarGridSpec(
            num_scalar_prefetch=2,
            grid=(calls // per,),
            in_specs=[unit] + piece_specs + [KEPT(a) for a in weights] + ([ANY] if aliased else []),
            out_specs=unit,
            scratch_shapes=[
                pltpu.VMEM((per * places, HW), jnp.bfloat16),
                pltpu.VMEM((per * places, width), jnp.bfloat16),
                pltpu.VMEM((per * places, 3 * HW), jnp.bfloat16),
            ],
        ),
        out_shape=jax.ShapeDtypeStruct(tokens.shape, jnp.bfloat16),
        input_output_aliases={len(operands) - 1: 0} if aliased else {},
        compiler_params=pltpu.CompilerParams(vmem_limit_bytes=VMEM_LIMIT),
        cost_estimate=pl.CostEstimate(
            flops=4 * calls * places * width * 5 * HW, bytes_accessed=8_000_000, transcendentals=0
        ),
        name="space_block",
    )(*operands)


def pack_kernel(route, slot, counts, x_ref, *refs):
    outs = refs[:-3]
    held, in_sems, out_sems = refs[-3:]
    devices, count = route.devices, route.count
    first = 0 if route.whole else 1
    clip = clip_at(slot, counts)
    loads, stores = [], []
    for k in range(first, devices):
        start = pl.multiple_of(block_start(route.peer(lax.axis_index("frame"), k), count, x_ref.shape[2]), ROWS)
        loads.append(pltpu.make_async_copy(x_ref.at[clip, :, pl.ds(start, count), :], held.at[k], in_sems.at[k]))
        target = outs[0].at[k] if route.whole else outs[k - first]
        stores.append(pltpu.make_async_copy(held.at[k], target, out_sems.at[k]))
    for load in loads:
        load.start()
    for load, store in zip(loads, stores):
        load.wait()
        store.start()
    for store in stores:
        store.wait()


def pack_step(route, slot, frame_count, tokens):
    _, frames, _, width = tokens.shape
    devices, count = route.devices, route.count
    if route.whole:
        out_shape = [jax.ShapeDtypeStruct((devices, frames, count, width), jnp.bfloat16)]
    else:
        out_shape = [jax.ShapeDtypeStruct((frames, count, width), jnp.bfloat16)] * (devices - 1)
    return pl.pallas_call(
        functools.partial(pack_kernel, route, slot),
        in_specs=[pl.BlockSpec(memory_space=pltpu.SMEM), ANY],
        out_specs=[ANY] * len(out_shape),
        out_shape=out_shape,
        scratch_shapes=[
            pltpu.VMEM((devices, frames, count, width), jnp.bfloat16),
            pltpu.SemaphoreType.DMA((devices,)),
            pltpu.SemaphoreType.DMA((devices,)),
        ],
        compiler_params=pltpu.CompilerParams(vmem_limit_bytes=VMEM_LIMIT),
        name="pack_tokens",
    )(frame_count, tokens)


def exchange_all(block):
    return lax.all_to_all(block, "frame", 0, 0, tiled=True)


def exchange(block, devices, k):
    return lax.ppermute(block, "frame", [(i, i ^ k) for i in range(devices)])


def far_and_near(devices):
    half = devices // 2
    order = []
    for k in range(half):
        order += [half + k, k + 1]
    return order[: devices - 1]


def per_device(
    devices,
    video_tokens,
    frame_count,
    token_count,
    time_gain,
    time_qkv,
    time_out,
    space_gain,
    space_qkv,
    space_out,
):
    _, frames, places, _ = video_tokens.shape
    time_weights = (time_gain[None, :], time_qkv)
    space_weights = (space_gain[None, :], time_out, space_qkv, space_out)
    counts = (frame_count, token_count)
    one = Route(True, devices, places // devices)
    two = Route(False, devices, places // devices)
    order = far_and_near(devices)

    (sent_a,) = pack_step(one, 0, frame_count, video_tokens)
    got_a = exchange_all(sent_a)
    sent_b = pack_step(two, 1, frame_count, video_tokens)
    sent_b, _ = lax.optimization_barrier((sent_b, got_a))
    got_b = {k: exchange(sent_b[k - 1], devices, k) for k in order}
    att_a = time_step(one, two, 0, frame_count, video_tokens, got_a, *time_weights)
    earlier = [got_b[k] for k in order]
    back_a = {}
    for place, k in enumerate(order):
        block, _ = lax.optimization_barrier((att_a[k], earlier[: place + LEAD]))
        back_a[k] = exchange(block, devices, k)
        earlier.append(back_a[k])
    received = [got_b[k] for k in range(1, devices)]
    (att_b,) = time_step(two, one, 1, frame_count, video_tokens, received, *time_weights)
    att_b, _ = lax.optimization_barrier((att_b, earlier[: len(order) + TAIL]))
    back_b = exchange_all(att_b)
    back_a = [att_a[0]] + [back_a[k] for k in range(1, devices)]
    out = space_step(two, 0, counts, video_tokens, back_a, 0, 0, frames, space_weights, None)
    return space_step(one, 1, counts, video_tokens, [back_b], 0, 0, frames, space_weights, out)


def solution(mesh):
    placed = (P("clip", "frame", None, None), P("clip"), P("clip"), P(), P(), P(), P(), P(), P())
    return jax.shard_map(
        functools.partial(per_device, mesh.shape["frame"]),
        mesh=mesh,
        in_specs=placed,
        out_specs=P("clip", "frame", None, None),
        check_vma=False,
    )
```
